1024 devices in a mesh: fsdp: 64 (over x, y_lo, core), dp: 16 (over y_hi, z).
Axes of the slice: x: 8, y: 8 (y_hi: 2, y_lo: 4; y = y_hi * 4 + y_lo), z: 8, core: 2. Of those that a mesh axis runs over, the one named last changes fastest.
Arguments:
- activations: bfloat16 [16, 16384, 4096], P('dp', 'fsdp'), may hold values from -16 to 16
- cotangents: bfloat16 [16, 16384, 512], P('dp', 'fsdp'), may hold values from -0.046875 to 0.046875
- momentum: float32 [16, 4096, 512], P('dp', 'fsdp'), may hold values from -6 to 6
- freq_index: int32 [256], replicated, may hold values from 0 to 4095, as said below
Outputs:
- new_momentum: float32 [16, 4096, 512], P('dp', 'fsdp')
- update: float32 [4096, 512], P('fsdp')
The draws below stay inside these ranges and needn't reach their ends.
Inputs may be any that keep to these rules, and one draw needn't show every extreme that they name: `freq_index`: 256 distinct indices in any order; 0 and 4095 are always among them.
All inputs are finite; a program needn't handle non-finite values.
Results may differ from the reference program's by a relative error of at most 0.0003.
Values sent between devices are 32-bit elements; how exact they have to be, the bound alone decides.
A program may use at most 128 MiB of HBM per device.

```python
import jax
import jax.numpy as jnp
from jax import lax

D = 4096
KVW = 512
BLOCK = 64
KEEP = 256
TOK_DEV = 256
TOK_GROUP = 16384
N_FSDP = 64
N_DP = 16


def draw_freq_index(key, part):
    first, second = jax.random.split(key)
    middle = jax.random.permutation(first, BLOCK * BLOCK - 2)[:KEEP - 2].astype(jnp.int32) + 1
    extremes = jnp.array([0, BLOCK * BLOCK - 1], dtype=jnp.int32)
    chosen = jnp.concatenate([extremes, middle])
    return jax.random.permutation(second, chosen).astype(jnp.int32)


def with_spikes(entries, key, source, target, shards_of, factor):
    owner, partner = [(jnp.arange(entries.shape[axis_at]) // (entries.shape[axis_at] // shards_of)).reshape([-1 if axis == axis_at else 1 for axis in range(entries.ndim)]) for axis_at in (source, target)]
    chosen = jax.random.permutation(key, shards_of)[partner]
    strong = (owner == chosen) | (owner == (partner + shards_of // 2) % shards_of)
    return jnp.where(strong, factor * entries, entries)


def level_of(key, extent, shards, low, top_value):
    loudness = 1.0
    for axis_at, shards_of in shards:
        draws = jax.random.uniform(jax.random.fold_in(jax.random.fold_in(key, 6), axis_at), (shards_of,), jnp.float32, low / len(shards), top_value / len(shards))
        loudness = loudness * jnp.repeat(jnp.exp(draws), extent[axis_at] // shards_of).reshape((-1,) + (1,) * (len(extent) - 1 - axis_at))
    return loudness


def gaussian(rng, shape, scale, limit, cuts=(), kind=jnp.bfloat16):
    loudness = level_of(rng, shape, cuts, -0.22, 0.18) if cuts else 1.0
    values = jax.random.normal(rng, shape, jnp.float32) * scale * loudness
    return jnp.minimum(jnp.maximum(values, -limit), limit).astype(kind)


def heavy_noise(rng, shape, spread, most, shards, heavy, kind=jnp.bfloat16):
    values = spread * jax.random.normal(rng, shape, jnp.float32)
    if shards:
        values = values * level_of(rng, shape, shards, -0.22, 0.18)
    return jnp.clip(with_spikes(values, jax.random.fold_in(rng, 3), *heavy), -most, most).astype(kind)


def setup_inputs(seed: int = 0) -> dict:
    key_list = jax.random.split(jax.random.key(seed), 5)
    return {
        "activations": heavy_noise(key_list[0], (N_DP, TOK_GROUP, D), 1.0, 16.0, ((0, 16), (1, 64)), (1, 2, 64, 4.0)),
        "cotangents": gaussian(key_list[1], (N_DP, TOK_GROUP, KVW), (1.0 / (TOK_DEV * N_FSDP) ** 0.5), 0.046875, ((0, 16), (1, 64))),
        "momentum": gaussian(key_list[2], (N_DP, D, KVW), 1.0, 6.0, ((0, 16), (1, 64)), jnp.float32),
        "freq_index": draw_freq_index(jax.random.fold_in(key_list[4], 71), 0),
    }


momentum_decay = 0.999

def cosine_basis(side):
    wave = jnp.arange(side, dtype=jnp.float32)[:, None]
    sample = jnp.arange(side, dtype=jnp.float32)[None, :]
    factor = jnp.where(wave == 0.0, jnp.sqrt(jnp.float32(1.0) / side), jnp.sqrt(jnp.float32(2.0) / side))
    return (factor * jnp.cos(jnp.pi * (2.0 * sample + 1.0) * wave / (2.0 * side))).astype(jnp.float32)

def forward(matrix, basis_mat):
    row_count, col_count = matrix.shape
    blocks = matrix.reshape(row_count // BLOCK, BLOCK, col_count // BLOCK, BLOCK)
    result = jnp.einsum('ka,iajb,lb->ikjl', basis_mat, blocks, basis_mat, precision=lax.Precision.HIGHEST)
    return result.reshape(row_count, col_count)

def inverse(matrix, basis_mat):
    row_count, col_count = matrix.shape
    blocks = matrix.reshape(row_count // BLOCK, BLOCK, col_count // BLOCK, BLOCK)
    result = jnp.einsum('ka,ikjl,lb->iajb', basis_mat, blocks, basis_mat, precision=lax.Precision.HIGHEST)
    return result.reshape(row_count, col_count)

def select_coeffs(coeffs, freq_index):
    row_count, col_count = coeffs.shape
    blocks = coeffs.reshape(row_count // BLOCK, BLOCK, col_count // BLOCK, BLOCK)
    wave_row = freq_index // BLOCK
    wave_col = freq_index % BLOCK
    return jnp.moveaxis(blocks[:, wave_row, :, wave_col], 0, -1)

def drop_selected(coeffs, freq_index):
    row_count, col_count = coeffs.shape
    flat_ids = jnp.arange(BLOCK * BLOCK, dtype=jnp.int32)
    taken = jnp.any(flat_ids[None, :] == freq_index[:, None], axis=0)
    keeper = 1.0 - taken.reshape(BLOCK, BLOCK).astype(jnp.float32)
    blocks = coeffs.reshape(row_count // BLOCK, BLOCK, col_count // BLOCK, BLOCK)
    return (blocks * keeper[None, :, None, :]).reshape(row_count, col_count)

def scatter_back(values, freq_index, row_count, col_count):
    wave_row = freq_index // BLOCK
    wave_col = freq_index % BLOCK
    blocks = jnp.zeros((row_count // BLOCK, BLOCK, col_count // BLOCK, BLOCK), jnp.float32)
    blocks = blocks.at[:, wave_row, :, wave_col].set(jnp.moveaxis(values, -1, 0))
    return blocks.reshape(row_count, col_count)

def reference(activations, cotangents, momentum, freq_index):
    basis_mat = cosine_basis(BLOCK)
    row_count = momentum.shape[1]
    col_count = momentum.shape[2]
    summed = jnp.zeros((row_count // BLOCK, col_count // BLOCK, KEEP), jnp.float32)
    states = []
    for group in range(N_DP):
        gradient = jnp.dot(activations[group].T, cotangents[group], preferred_element_type=jnp.float32)
        fresh = momentum_decay * momentum[group] + gradient
        coeffs = forward(fresh, basis_mat)
        summed = summed + select_coeffs(coeffs, freq_index)
        states.append(inverse(drop_selected(coeffs, freq_index), basis_mat))
    new_momentum = jnp.stack(states, axis=0)
    update = inverse(scatter_back(summed / N_DP, freq_index, row_count, col_count), basis_mat)
    return (new_momentum, update)
```

```python
import jax
import jax.numpy as jnp
import ml_dtypes
import numpy as np
from jax import lax
from jax.experimental import pallas as pl
from jax.experimental.pallas import tpu as pltpu
from jax.sharding import PartitionSpec as P

BLOCK = 64
KEEP = 256
NX = 8
NY = 4
NDP = 16
TOK = 256
COLS = 512
ROWS_A = 40
ROWS_B = BLOCK - ROWS_A
HALF_B = 16
MOMENTUM_DECAY = 0.999
BF16 = jnp.bfloat16
F32 = jnp.float32


def basis_tables():
    wave = np.arange(BLOCK)[:, None]
    sample = np.arange(BLOCK)[None, :]
    phase = ((2 * sample + 1) * wave) % (4 * BLOCK)
    scale = np.where(wave == 0, np.sqrt(1.0 / BLOCK), np.sqrt(2.0 / BLOCK))
    basis = scale * np.cos(np.pi * phase / (2.0 * BLOCK))
    high = basis.astype(ml_dtypes.bfloat16)
    low = (basis - high.astype(np.float64)).astype(ml_dtypes.bfloat16)
    return np.concatenate([high, low, high, low, high, high, low, low], axis=1)


def dot(lhs, rhs, left=1, right=0):
    return lax.dot_general(lhs, rhs, (((left,), (right,)), ((), ())), preferred_element_type=F32)


def split(values):
    high = values.astype(BF16)
    return high, (values - high.astype(F32)).astype(BF16)


def slot_of(step, way):
    if step == 1:
        return 0
    if step == 5:
        return 7
    return 2 * (step - 1) - 1 + way


def kernel(
    act, cot, mom, freq, table, newm, upd,
    act_v, cot_v, mom_v, cot_send, cot_recv, cot_peer,
    pick_send, pick_recv, kept, ga, gb, rax, ray, rby, rbx,
    rmix, rinv, ltile, pall,
    load_sem, cot_load_sem, mom_sem,
    core_send, core_recv, cot_sem,
    axs, axr, ays, ayr, bys, byr, bxs, bxr, dps, dpr,
):
    me = lax.axis_index("fsdp")
    dp = lax.axis_index("dp")
    x = me // (2 * NY)
    y = (me // 2) % NY
    core = me % 2
    base = me - 2 * NY * x
    peer = me + 1 - 2 * core
    around = (lax.rem(x + 1, NX) * (2 * NY) + base, lax.rem(x + NX - 1, NX) * (2 * NY) + base)
    inner_right = y < NY - 1
    inner_left = y > 0
    along = (jnp.where(inner_right, me + 2, me - 2), jnp.where(inner_left, me - 2, me + 2))

    def slot_x(i):
        far = 4 - (i + 1) // 2
        return lax.rem(x + jnp.where(i % 2 == 1, far, NX - far), NX)

    def load(i):
        start = pl.multiple_of(slot_x(i) * COLS, COLS)
        return pltpu.make_async_copy(act.at[0, :, pl.ds(start, COLS)], act_v.at[i], load_sem.at[i])

    cot_load = pltpu.make_async_copy(cot.at[0], cot_v, cot_load_sem)
    mom_load = pltpu.make_async_copy(mom.at[0], mom_v, mom_sem)
    cot_load.start()
    for i in range(NX):
        load(jnp.int32(i)).start()
    mom_load.start()

    barrier = pltpu.get_barrier_semaphore()

    def hello(where):
        pl.semaphore_signal(barrier, inc=1, device_id=where, device_id_type=pl.DeviceIdType.MESH)

    hello({"fsdp": peer})
    hello({"fsdp": around[0]})
    hello({"fsdp": around[1]})

    @pl.when(inner_right)
    def _():
        hello({"fsdp": along[0]})

    @pl.when(inner_left)
    def _():
        hello({"fsdp": along[1]})

    def hello_group(j, carry):
        hello({"dp": lax.rem(dp + j, NDP)})
        return carry

    lax.fori_loop(1, NDP, hello_group, 0)

    out_row = lax.broadcasted_iota(jnp.int32, (TOK, COLS), 0)
    in_col = lax.broadcasted_iota(jnp.int32, (TOK, COLS), 1)
    wanted = (out_row // BLOCK) * (2 * BLOCK) + out_row % BLOCK
    take_kept = jnp.where(in_col == wanted + core * BLOCK, 1.0, 0.0).astype(BF16)
    take_sent = jnp.where(in_col == wanted + (1 - core) * BLOCK, 1.0, 0.0).astype(BF16)

    cot_load.wait()
    cot_send[...] = cot_v[...].astype(F32)
    pl.semaphore_wait(
        barrier, 3 + (NDP - 1) + inner_right.astype(jnp.int32) + inner_left.astype(jnp.int32)
    )

    def send(src, dst, send_sem, recv_sem, where):
        return pltpu.make_async_remote_copy(
            src_ref=src, dst_ref=dst, send_sem=send_sem, recv_sem=recv_sem,
            device_id=where, device_id_type=pl.DeviceIdType.MESH,
        )

    cot_copy = send(cot_send, cot_recv, cot_sem.at[0], cot_sem.at[1], {"fsdp": peer})
    cot_copy.start()

    def swap(i):
        return send(pick_send.at[i], pick_recv.at[i], core_send.at[i], core_recv.at[i], {"fsdp": peer})

    def exchange(i, carry):
        load(i).wait()
        block = act_v[i]
        pick_send[i] = dot(take_sent, block, 1, 1)
        swap(i).start()
        kept[i] = dot(take_kept, block, 1, 1).astype(BF16)
        return carry

    lax.fori_loop(0, NX, exchange, 0)

    def ax_copy(way, step, sub):
        return send(
            ga.at[slot_of(step, way), sub], rax.at[way, step - 1, sub],
            axs.at[way, step - 1, sub], axr.at[way, step - 1, sub], {"fsdp": around[way]},
        )

    def ay_copy(way, owner):
        return send(
            ga.at[7, owner], ray.at[way, owner], ays.at[owner], ayr.at[way, owner],
            {"fsdp": along[way]},
        )

    def by_copy(way, i, owner):
        return send(
            gb.at[i, owner], rby.at[way, i, owner], bys.at[i, owner], byr.at[way, i, owner],
            {"fsdp": along[way]},
        )

    def bx_copy(way, step):
        slot = slot_of(step, way)
        if step == 1:
            rows = pl.ds(0, HALF_B) if way == 0 else pl.ds(HALF_B, ROWS_B - HALF_B)
        else:
            rows = pl.ds(0, ROWS_B)
        return send(
            gb.at[slot, y, rows], rbx.at[way, step - 1, rows],
            bxs.at[way, step - 1], bxr.at[way, step - 1], {"fsdp": around[way]},
        )

    def first_half(way, sub):
        return (sub < 2) == (way == 0)

    cot_copy.wait_recv()
    cot_peer[...] = cot_recv[...].astype(BF16)

    def product(i, carry):
        total = dot(kept[i], cot_v[...])
        swap(i).wait_recv()
        total = total + dot(pick_recv[i].astype(BF16), cot_peer[...])
        blocks = total.reshape(NY, BLOCK, COLS)
        ga[i] = blocks[:, :ROWS_A]
        gb[i] = blocks[:, ROWS_A:]

        @pl.when(i == 0)
        def _():
            for sub in range(2):
                ax_copy(0, 1, sub).start()
                ax_copy(1, 1, sub + 2).start()

        @pl.when(i == 1)
        def _():
            for sub in (2, 3):
                ax_copy(0, 2, sub).start()

        @pl.when(i == 2)
        def _():
            for sub in (0, 1):
                ax_copy(1, 2, sub).start()

        @pl.when(y == 0)
        def _():
            for owner in (3, 2, 1):
                by_copy(0, i, owner).start()

        @pl.when(y == NY - 1)
        def _():
            for owner in (0, 1, 2):
                by_copy(1, i, owner).start()

        return carry

    lax.fori_loop(0, NX, product, 0)

    wave = lax.broadcasted_iota(jnp.int32, (BLOCK, KEEP), 0)
    chosen = freq[...]
    hot_row = jnp.where(wave == chosen // BLOCK, 1.0, 0.0).astype(BF16)
    hot_col = jnp.where(wave == chosen % BLOCK, 1.0, 0.0).astype(BF16)
    rmix[...] = dot(hot_row, table[:, :256], 0, 0).astype(BF16)
    rinv[...] = dot(table[:, :128], hot_row, 0, 0).astype(BF16)
    pair = dot(hot_col, table[:, 256:], 0, 0)
    narrow = pair[:, :128] + pair[:, 128:]
    ltile[...] = jnp.concatenate([narrow] * 4, axis=1)

    def ax_round(step, sub):
        for way in (0, 1):
            if step == 2 and not first_half(way, sub):
                continue
            ax_copy(way, step - 1, sub).wait_recv()
            slot = slot_of(step, way)
            ga[slot, sub] = ga[slot, sub] + rax[way, step - 2, sub]
            if step <= 4:
                ax_copy(way, step, sub).start()

    def chain_y(total, arrived, copy):
        for k in range(NY - 2):
            right, left = NY - 1 - k, k

            @pl.when(inner_left & (y < right))
            def _(owner=right):
                copy(0, owner).wait_recv()
                total(owner)[...] = total(owner)[...] + arrived(0, owner)[...]
                copy(0, owner).start()

            @pl.when(inner_right & (y > left))
            def _(owner=left):
                copy(1, owner).wait_recv()
                total(owner)[...] = total(owner)[...] + arrived(1, owner)[...]
                copy(1, owner).start()

        @pl.when(inner_left)
        def _():
            copy(0, y).wait_recv()
            total(y)[...] = total(y)[...] + arrived(0, y)[...]

        @pl.when(inner_right)
        def _():
            copy(1, y).wait_recv()
            total(y)[...] = total(y)[...] + arrived(1, y)[...]

    def bx_round(i):
        if i == 0:
            bx_copy(0, 1).start()
            bx_copy(1, 1).start()
            return
        ways = (0, 1) if i == 7 else ((i + 1) % 2,)
        step = (i + 1) // 2 + 1
        for way in ways:
            bx_copy(way, step - 1).wait_recv()
            if step == 2:
                rows = pl.ds(0, HALF_B) if way == 0 else pl.ds(HALF_B, ROWS_B - HALF_B)
            else:
                rows = pl.ds(0, ROWS_B)
            gb[i, y, rows] = gb[i, y, rows] + rbx[way, step - 2, rows]
            if step <= 4:
                bx_copy(way, step).start()

    rounds = [(2, (0, 2)), (2, (1, 3))] + [(s, (q,)) for s in (3, 4, 5) for q in range(NY)]
    counts = [2, 2, 2, 2, 2, 2, 1, 1]
    at = 0
    for i in range(NX):
        chain_y(
            lambda o, i=i: gb.at[i, o], lambda w, o, i=i: rby.at[w, i, o],
            lambda w, o, i=i: by_copy(w, i, o),
        )
        for step, subs in rounds[at:at + counts[i]]:
            for sub in subs:
                ax_round(step, sub)
        at += counts[i]
        if i > 0:
            bx_round(i - 1)

    @pl.when(y == 0)
    def _():
        for owner in (3, 2, 1):
            ay_copy(0, owner).start()

    @pl.when(y == NY - 1)
    def _():
        for owner in (0, 1, 2):
            ay_copy(1, owner).start()

    chain_y(lambda o: ga.at[7, o], lambda w, o: ray.at[w, o], ay_copy)
    bx_round(7)

    mom_load.wait()
    gradient = jnp.concatenate([ga[7, y], gb[7, y]], axis=0)
    fresh = MOMENTUM_DECAY * mom_v[...] + gradient
    high, low = split(fresh)
    spread = dot(rmix[...], jnp.concatenate([high, high, low, low], axis=0)) * ltile[...]
    high, low = split(spread)
    block_row = lax.broadcasted_iota(jnp.int32, (8, COLS), 0)
    block_col = lax.broadcasted_iota(jnp.int32, (8, COLS), 1)
    ones = jnp.where(block_col // BLOCK == block_row, 1.0, 0.0).astype(BF16)
    picks = dot(ones, high, 1, 1) + dot(ones, low, 1, 1)
    pall[dp] = picks

    def dp_copy(to, slot):
        return send(pall.at[slot], pall.at[slot], dps.at[to], dpr.at[slot], {"dp": to})

    def share(j, carry):
        dp_copy(lax.rem(dp + j, NDP), dp).start()
        return carry

    lax.fori_loop(1, NDP, share, 0)

    def back(values):
        high, low = split(values)
        wide = dot(jnp.concatenate([high, low], axis=0), jnp.concatenate([ones, ones], axis=0), 0, 0)
        high, low = split(wide * ltile[...])
        both = dot(rinv[...], high)
        return both[:BLOCK] + both[BLOCK:] + dot(rinv[:BLOCK, :], low)

    newm[0] = fresh - back(picks)

    def gather(j, carry):
        other = lax.rem(dp + j, NDP)
        dp_copy(other, other).wait_recv()
        return carry

    lax.fori_loop(1, NDP, gather, 0)
    upd[...] = back(jnp.sum(pall[...], axis=0) * (1.0 / NDP))

    cot_copy.wait_send()

    def done_core(i, carry):
        swap(i).wait_send()
        return carry

    lax.fori_loop(0, NX, done_core, 0)
    for way in (0, 1):
        for step in range(1, 5):
            for sub in range(NY):
                if step > 1 or first_half(way, sub):
                    ax_copy(way, step, sub).wait_send()
            bx_copy(way, step).wait_send()
    for owner in range(NY):

        @pl.when(y != owner)
        def _(owner=owner):
            ay_copy(0, owner).wait_send()

            def done_y(i, carry):
                by_copy(0, i, owner).wait_send()
                return carry

            lax.fori_loop(0, NX, done_y, 0)

    def done_dp(j, carry):
        dp_copy(lax.rem(dp + j, NDP), dp).wait_send()
        return carry

    lax.fori_loop(1, NDP, done_dp, 0)


def shards(activations, cotangents, momentum, freq_index):
    vmem = pl.BlockSpec(memory_space=pltpu.VMEM)
    hbm = pl.BlockSpec(memory_space=pl.ANY)
    dma = pltpu.SemaphoreType.DMA
    return pl.pallas_call(
        kernel,
        out_shape=(
            jax.ShapeDtypeStruct((1, BLOCK, COLS), F32),
            jax.ShapeDtypeStruct((BLOCK, COLS), F32),
        ),
        in_specs=[hbm, hbm, hbm, vmem, vmem],
        out_specs=(vmem, vmem),
        scratch_shapes=[
            pltpu.VMEM((NX, TOK, COLS), BF16),
            pltpu.VMEM((TOK, COLS), BF16),
            pltpu.VMEM((BLOCK, COLS), F32),
            pltpu.VMEM((TOK, COLS), F32),
            pltpu.VMEM((TOK, COLS), F32),
            pltpu.VMEM((TOK, COLS), BF16),
            pltpu.VMEM((NX, NY * BLOCK, TOK), F32),
            pltpu.VMEM((NX, NY * BLOCK, TOK), F32),
            pltpu.VMEM((NX, NY * BLOCK, TOK), BF16),
            pltpu.VMEM((NX, NY, ROWS_A, COLS), F32),
            pltpu.VMEM((NX, NY, ROWS_B, COLS), F32),
            pltpu.VMEM((2, 4, NY, ROWS_A, COLS), F32),
            pltpu.VMEM((2, NY, ROWS_A, COLS), F32),
            pltpu.VMEM((2, NX, NY, ROWS_B, COLS), F32),
            pltpu.VMEM((2, 4, ROWS_B, COLS), F32),
            pltpu.VMEM((KEEP, 256), BF16),
            pltpu.VMEM((128, KEEP), BF16),
            pltpu.VMEM((KEEP, COLS), F32),
            pltpu.VMEM((NDP, 8, KEEP), F32),
            dma((NX,)), dma, dma,
            dma((NX,)), dma((NX,)), dma((2,)),
            dma((2, 4, NY)), dma((2, 4, NY)),
            dma((NY,)), dma((2, NY)),
            dma((NX, NY)), dma((2, NX, NY)),
            dma((2, 4)), dma((2, 4)),
            dma((NDP,)), dma((NDP,)),
        ],
        compiler_params=pltpu.CompilerParams(
            collective_id=0, has_side_effects=True, vmem_limit_bytes=48 * 1024 * 1024
        ),
    )(activations, cotangents, momentum, freq_index.reshape(1, KEEP), jnp.asarray(basis_tables()))


def solution(mesh):
    return jax.shard_map(
        shards,
        mesh=mesh,
        in_specs=(P("dp", "fsdp", None), P("dp", "fsdp", None), P("dp", "fsdp", None), P()),
        out_specs=(P("dp", "fsdp", None), P("fsdp", None)),
        check_vma=False,
    )
```

```python
import jax
import jax.numpy as jnp
import ml_dtypes
import numpy as np
from jax import lax
from jax.experimental import pallas as pl
from jax.experimental.pallas import tpu as pltpu
from jax.sharding import PartitionSpec as P

BLOCK = 64
KEEP = 256
NX = 8
NY = 4
NDP = 16
TOK = 256
COLS = 512
ROWS_A = 48
ROWS_B = BLOCK - ROWS_A
HALF_B = 8
MOMENTUM_DECAY = 0.999
BF16 = jnp.bfloat16
F32 = jnp.float32


def basis_tables():
    wave = np.arange(BLOCK)[:, None]
    sample = np.arange(BLOCK)[None, :]
    phase = ((2 * sample + 1) * wave) % (4 * BLOCK)
    scale = np.where(wave == 0, np.sqrt(1.0 / BLOCK), np.sqrt(2.0 / BLOCK))
    basis = scale * np.cos(np.pi * phase / (2.0 * BLOCK))
    high = basis.astype(ml_dtypes.bfloat16)
    low = (basis - high.astype(np.float64)).astype(ml_dtypes.bfloat16)
    return np.concatenate([high, low, high, low, high, high, low, low], axis=1)


def dot(lhs, rhs, left=1, right=0):
    return lax.dot_general(lhs, rhs, (((left,), (right,)), ((), ())), preferred_element_type=F32)


def split(values):
    high = values.astype(BF16)
    return high, (values - high.astype(F32)).astype(BF16)


def slot_of(step, way):
    if step == 1:
        return 0
    if step == 5:
        return 7
    return 2 * (step - 1) - 1 + way


def kernel(
    act, cot, mom, freq, table, newm, upd,
    act_v, cot_v, mom_v, freq_v, table_v, take_kept, take_sent, cot_send, cot_recv, cot_peer,
    pick_send, pick_recv, kept, ga, gb, rax, ray, rby, rbx,
    rmix, rinv, ltile, pall,
    load_sem, small_sem, core_send, core_recv, cot_sem,
    axs, axr, ays, ayr, bys, byr, bxs, bxr, dps, dpr,
):
    me = lax.axis_index("fsdp")
    dp = lax.axis_index("dp")
    x = me // (2 * NY)
    y = (me // 2) % NY
    core = me % 2
    base = me - 2 * NY * x
    peer = me + 1 - 2 * core
    around = (lax.rem(x + 1, NX) * (2 * NY) + base, lax.rem(x + NX - 1, NX) * (2 * NY) + base)

    def ranked(rank):
        return lax.rem(y + 1 + rank, NY)

    def slot_x(i):
        far = 4 - (i + 1) // 2
        return lax.rem(x + jnp.where(i % 2 == 1, far, NX - far), NX)

    def load(i):
        start = pl.multiple_of(slot_x(i) * COLS, COLS)
        return pltpu.make_async_copy(act.at[0, :, pl.ds(start, COLS)], act_v.at[i], load_sem.at[i])

    cot_load = pltpu.make_async_copy(cot.at[0], cot_v, small_sem.at[0])
    mom_load = pltpu.make_async_copy(mom.at[0], mom_v, small_sem.at[1])
    freq_load = pltpu.make_async_copy(freq, freq_v, small_sem.at[2])
    table_load = pltpu.make_async_copy(table, table_v, small_sem.at[3])
    cot_load.start()
    for i in range(NX):
        load(jnp.int32(i)).start()
    freq_load.start()
    table_load.start()
    mom_load.start()

    barrier = pltpu.get_barrier_semaphore()

    def hello(where):
        pl.semaphore_signal(barrier, inc=1, device_id=where, device_id_type=pl.DeviceIdType.MESH)

    def hello_group(j, carry):
        hello({"dp": lax.rem(dp + j, NDP)})
        return carry

    lax.fori_loop(1, NDP, hello_group, 0)
    for rank in range(NY - 1):
        hello({"fsdp": me + 2 * (ranked(rank) - y)})
    hello({"fsdp": around[0]})
    hello({"fsdp": around[1]})
    hello({"fsdp": peer})

    out_row = lax.broadcasted_iota(jnp.int32, (TOK, COLS), 0)
    in_col = lax.broadcasted_iota(jnp.int32, (TOK, COLS), 1)
    wanted = (out_row // BLOCK) * (2 * BLOCK) + out_row % BLOCK
    take_kept[...] = jnp.where(in_col == wanted + core * BLOCK, 1.0, 0.0).astype(BF16)
    take_sent[...] = jnp.where(in_col == wanted + (1 - core) * BLOCK, 1.0, 0.0).astype(BF16)

    def send(src, dst, send_sem, recv_sem, where):
        return pltpu.make_async_remote_copy(
            src_ref=src, dst_ref=dst, send_sem=send_sem, recv_sem=recv_sem,
            device_id=where, device_id_type=pl.DeviceIdType.MESH,
        )

    cot_copy = send(cot_send, cot_recv, cot_sem.at[0], cot_sem.at[1], {"fsdp": peer})

    def swap(i):
        return send(pick_send.at[i], pick_recv.at[i], core_send.at[i], core_recv.at[i], {"fsdp": peer})

    def pick(i):
        load(i).wait()
        pick_send[i] = dot(take_sent[...], act_v[i], 1, 1)

    def keep(i):
        kept[i] = dot(take_kept[...], act_v[i], 1, 1).astype(BF16)

    def ax_copy(way, step, rank):
        sub = ranked(rank)
        return send(
            ga.at[slot_of(step, way), sub], rax.at[way, step - 1, rank],
            axs.at[way, step - 1, rank], axr.at[way, step - 1, rank], {"fsdp": around[way]},
        )

    def to_line(rank):
        return {"fsdp": me + 2 * (ranked(rank) - y)}

    def ay_copy(rank):
        return send(
            ga.at[NX - 1, ranked(rank)], ray.at[rank], ays.at[rank], ayr.at[rank], to_line(rank)
        )

    def by_copy(i, rank):
        return send(
            gb.at[i, ranked(rank)], rby.at[i, rank], bys.at[i, rank], byr.at[i, rank], to_line(rank)
        )

    def bx_rows(way, step):
        if step > 1:
            return pl.ds(0, ROWS_B)
        return pl.ds(0, HALF_B) if way == 0 else pl.ds(HALF_B, ROWS_B - HALF_B)

    def bx_copy(way, step):
        rows = bx_rows(way, step)
        return send(
            gb.at[slot_of(step, way), y, rows], rbx.at[way, step - 1, rows],
            bxs.at[way, step - 1], bxr.at[way, step - 1], {"fsdp": around[way]},
        )

    def first_half(way, rank):
        return (rank < 2) == (way == 0)

    def product(i):
        total = dot(kept[i], cot_v[...])
        swap(i).wait_recv()
        total = total + dot(pick_recv[i].astype(BF16), cot_peer[...])
        blocks = total.reshape(NY, BLOCK, COLS)
        ga[i] = blocks[:, :ROWS_A]
        gb[i] = blocks[:, ROWS_A:]

    def by_start(i):
        for rank in range(NY - 1):
            by_copy(i, rank).start()

    cot_load.wait()
    cot_send[...] = cot_v[...].astype(F32)
    pick(jnp.int32(0))
    pl.semaphore_wait(barrier, 3 + (NY - 1) + (NDP - 1))
    cot_copy.start()
    swap(0).start()
    keep(0)
    for i in (1, 2):
        pick(jnp.int32(i))
        swap(i).start()
        keep(i)
    cot_copy.wait_recv()
    cot_peer[...] = cot_recv[...].astype(BF16)

    product(0)
    for rank in (0, 1):
        ax_copy(0, 1, rank).start()
        ax_copy(1, 1, rank + 2).start()
    by_start(0)
    product(1)
    for rank in (2, 3):
        ax_copy(0, 2, rank).start()
    product(2)
    for rank in (0, 1):
        ax_copy(1, 2, rank).start()
    by_start(1)
    by_start(2)

    def stage(i, carry):
        pick(i)
        swap(i).start()
        keep(i)
        return carry

    lax.fori_loop(3, NX, stage, 0)

    def finish(i, carry):
        product(i)
        by_start(i)
        return carry

    lax.fori_loop(3, NX, finish, 0)

    def choose():
        freq_load.wait()
        table_load.wait()
        wave = lax.broadcasted_iota(jnp.int32, (BLOCK, KEEP), 0)
        chosen = freq_v[...]
        hot_row = jnp.where(wave == chosen // BLOCK, 1.0, 0.0).astype(BF16)
        hot_col = jnp.where(wave == chosen % BLOCK, 1.0, 0.0).astype(BF16)
        rmix[...] = dot(hot_row, table_v[:, :256], 0, 0).astype(BF16)
        rinv[...] = dot(table_v[:, :128], hot_row, 0, 0).astype(BF16)
        pair = dot(hot_col, table_v[:, 256:], 0, 0)
        narrow = pair[:, :128] + pair[:, 128:]
        ltile[...] = jnp.concatenate([narrow] * 4, axis=1)

    def ax_part(way, step, rank):
        ax_copy(way, step - 1, rank).wait_recv()
        slot, sub = slot_of(step, way), ranked(rank)
        ga[slot, sub] = ga[slot, sub] + rax[way, step - 2, rank]
        if step <= 4:
            ax_copy(way, step, rank).start()

    orders = {2: ((0, 1), (2, 3)), 3: ((2, 0, 3, 1), (0, 2, 1, 3)), 4: ((0, 2, 1, 3),) * 2, 5: ((0, 2, 1, 3),) * 2}

    def ax_round(step, place):
        for way in (0, 1):
            ax_part(way, step, orders[step][way][place])
        if step == 5 and place < 3:
            ay_copy(orders[5][0][place]).start()

    def by_round(i):
        total = gb[i, y]
        for rank in range(NY - 1):
            by_copy(i, rank).wait_recv()
            total = total + rby[i, rank]
        gb[i, y] = total

    def bx_round(i):
        if i == 0:
            bx_copy(0, 1).start()
            bx_copy(1, 1).start()
            return
        ways = (0, 1) if i == 7 else ((i + 1) % 2,)
        step = (i + 1) // 2 + 1
        for way in ways:
            bx_copy(way, step - 1).wait_recv()
            rows = bx_rows(way, step - 1)
            gb[i, y, rows] = gb[i, y, rows] + rbx[way, step - 2, rows]
            if step <= 4:
                bx_copy(way, step).start()

    ax_round(2, 0)
    by_round(0)
    bx_round(0)
    ax_round(2, 1)
    by_round(1)
    ax_round(3, 0)
    choose()
    by_round(2)
    bx_round(1)
    bx_round(2)
    ax_round(3, 1)
    ax_round(3, 2)
    by_round(3)
    ax_round(3, 3)
    by_round(4)
    bx_round(3)
    bx_round(4)
    by_round(5)
    ax_round(4, 0)
    ax_round(4, 1)
    by_round(6)
    ax_round(4, 2)
    ax_round(4, 3)
    bx_round(5)
    bx_round(6)
    by_round(7)
    for place in range(NY):
        ax_round(5, place)
    bx_round(7)

    mom_load.wait()
    for rank in (0, 2, 1):
        ay_copy(rank).wait_recv()
    gradient = jnp.concatenate([ga[NX - 1, y] + (ray[0] + ray[1] + ray[2]), gb[NX - 1, y]], axis=0)
    fresh = MOMENTUM_DECAY * mom_v[...] + gradient
    high, low = split(fresh)
    spread = dot(rmix[...], jnp.concatenate([high, high, low, low], axis=0)) * ltile[...]
    high, low = split(spread)
    block_row = lax.broadcasted_iota(jnp.int32, (8, COLS), 0)
    block_col = lax.broadcasted_iota(jnp.int32, (8, COLS), 1)
    ones = jnp.where(block_col // BLOCK == block_row, 1.0, 0.0).astype(BF16)
    picks = dot(ones, high, 1, 1) + dot(ones, low, 1, 1)
    pall[dp] = picks

    def dp_copy(to, slot):
        return send(pall.at[slot], pall.at[slot], dps.at[to], dpr.at[slot], {"dp": to})

    def other(j):
        return lax.rem(dp + NDP // 2 + j, NDP)

    def share(j, carry):
        @pl.when(j != NDP // 2)
        def _():
            dp_copy(other(j), dp).start()

        return carry

    lax.fori_loop(0, NDP, share, 0)

    def back(values):
        high, low = split(values)
        wide = dot(jnp.concatenate([high, low], axis=0), jnp.concatenate([ones, ones], axis=0), 0, 0)
        high, low = split(wide * ltile[...])
        both = dot(rinv[...], high)
        return both[:BLOCK] + both[BLOCK:] + dot(rinv[:BLOCK, :], low)

    newm[0] = fresh - back(picks)

    cot_copy.wait_send()

    def done(i, carry):
        swap(i).wait_send()
        for rank in range(NY - 1):
            by_copy(i, rank).wait_send()
        return carry

    lax.fori_loop(0, NX, done, 0)
    for way in (0, 1):
        for step in range(1, 5):
            for rank in range(NY):
                if step > 1 or first_half(way, rank):
                    ax_copy(way, step, rank).wait_send()
            bx_copy(way, step).wait_send()
    for rank in range(NY - 1):
        ay_copy(rank).wait_send()

    def gather(j, carry):
        where = lax.rem(dp + j, NDP)
        dp_copy(where, where).wait_recv()
        return carry

    lax.fori_loop(1, NDP, gather, 0)
    upd[...] = back(jnp.sum(pall[...], axis=0) * (1.0 / NDP))

    def done_dp(j, carry):
        dp_copy(lax.rem(dp + j, NDP), dp).wait_send()
        return carry

    lax.fori_loop(1, NDP, done_dp, 0)


def shards(activations, cotangents, momentum, freq_index):
    vmem = pl.BlockSpec(memory_space=pltpu.VMEM)
    hbm = pl.BlockSpec(memory_space=pl.ANY)
    dma = pltpu.SemaphoreType.DMA
    return pl.pallas_call(
        kernel,
        out_shape=(
            jax.ShapeDtypeStruct((1, BLOCK, COLS), F32),
            jax.ShapeDtypeStruct((BLOCK, COLS), F32),
        ),
        in_specs=[hbm] * 5,
        out_specs=(vmem, vmem),
        scratch_shapes=[
            pltpu.VMEM((NX, TOK, COLS), BF16),
            pltpu.VMEM((TOK, COLS), BF16),
            pltpu.VMEM((BLOCK, COLS), F32),
            pltpu.VMEM((1, KEEP), jnp.int32),
            pltpu.VMEM((BLOCK, COLS), BF16),
            pltpu.VMEM((TOK, COLS), BF16),
            pltpu.VMEM((TOK, COLS), BF16),
            pltpu.VMEM((TOK, COLS), F32),
            pltpu.VMEM((TOK, COLS), F32),
            pltpu.VMEM((TOK, COLS), BF16),
            pltpu.VMEM((NX, NY * BLOCK, TOK), F32),
            pltpu.VMEM((NX, NY * BLOCK, TOK), F32),
            pltpu.VMEM((NX, NY * BLOCK, TOK), BF16),
            pltpu.VMEM((NX, NY, ROWS_A, COLS), F32),
            pltpu.VMEM((NX, NY, ROWS_B, COLS), F32),
            pltpu.VMEM((2, 4, NY, ROWS_A, COLS), F32),
            pltpu.VMEM((NY - 1, ROWS_A, COLS), F32),
            pltpu.VMEM((NX, NY - 1, ROWS_B, COLS), F32),
            pltpu.VMEM((2, 4, ROWS_B, COLS), F32),
            pltpu.VMEM((KEEP, 256), BF16),
            pltpu.VMEM((128, KEEP), BF16),
            pltpu.VMEM((KEEP, COLS), F32),
            pltpu.VMEM((NDP, 8, KEEP), F32),
            dma((NX,)), dma((4,)), dma((NX,)), dma((NX,)), dma((2,)),
            dma((2, 4, NY)), dma((2, 4, NY)),
            dma((NY - 1,)), dma((NY - 1,)),
            dma((NX, NY - 1)), dma((NX, NY - 1)),
            dma((2, 4)), dma((2, 4)),
            dma((NDP,)), dma((NDP,)),
        ],
        compiler_params=pltpu.CompilerParams(
            collective_id=0, has_side_effects=True, vmem_limit_bytes=62 * 1024 * 1024
        ),
    )(activations, cotangents, momentum, freq_index.reshape(1, KEEP), jnp.asarray(basis_tables()))


def solution(mesh):
    return jax.shard_map(
        shards,
        mesh=mesh,
        in_specs=(P("dp", "fsdp", None), P("dp", "fsdp", None), P("dp", "fsdp", None), P()),
        out_specs=(P("dp", "fsdp", None), P("fsdp", None)),
        check_vma=False,
    )
```

```python
import jax
import jax.numpy as jnp
import ml_dtypes
import numpy as np
from jax import lax
from jax.experimental import pallas as pl
from jax.experimental.pallas import tpu as pltpu
from jax.sharding import PartitionSpec as P

BLOCK = 64
KEEP = 256
NX = 8
NY = 4
NDP = 16
TOK = 256
COLS = 512
ROWS_A = 48
ROWS_B = BLOCK - ROWS_A
HALF_B = 8
MOMENTUM_DECAY = 0.999
BF16 = jnp.bfloat16
F32 = jnp.float32


def basis_tables():
    wave = np.arange(BLOCK)[:, None]
    sample = np.arange(BLOCK)[None, :]
    phase = ((2 * sample + 1) * wave) % (4 * BLOCK)
    scale = np.where(wave == 0, np.sqrt(1.0 / BLOCK), np.sqrt(2.0 / BLOCK))
    basis = scale * np.cos(np.pi * phase / (2.0 * BLOCK))
    high = basis.astype(ml_dtypes.bfloat16)
    low = (basis - high.astype(np.float64)).astype(ml_dtypes.bfloat16)
    return np.concatenate([high, low, high, low, high, high, low, low], axis=1)


def dot(lhs, rhs, left=1, right=0):
    return lax.dot_general(lhs, rhs, (((left,), (right,)), ((), ())), preferred_element_type=F32)


def split(values):
    high = values.astype(BF16)
    return high, (values - high.astype(F32)).astype(BF16)


def slot_of(step, way):
    if step == 1:
        return 0
    if step == 5:
        return 7
    return 2 * (step - 1) - 1 + way


def kernel(
    act, cot, mom, freq, table, newm, upd,
    act_v, cot_v, mom_v, freq_v, table_v, take_kept, take_sent, cot_send, cot_recv, cot_peer,
    pick_send, pick_recv, kept, ga, gb, rax, ray, rby, rbx,
    rmix, rinv, ltile, held, pg, psum, rpy, rpx, pall,
    gate, load_sem, small_sem, core_send, core_recv, cot_sem,
    axs, axr, ays, ayr, bys, byr, bxs, bxr, pys, pyr, pxs, pxr, dps, dpr,
):
    me = lax.axis_index("fsdp")
    dp = lax.axis_index("dp")
    x = me // (2 * NY)
    y = (me // 2) % NY
    core = me % 2
    base = me - 2 * NY * x
    peer = me + 1 - 2 * core
    around = (lax.rem(x + 1, NX) * (2 * NY) + base, lax.rem(x + NX - 1, NX) * (2 * NY) + base)

    def ranked(rank):
        return lax.rem(y + 1 + rank, NY)

    def slot_x(i):
        far = 4 - (i + 1) // 2
        return lax.rem(x + jnp.where(i % 2 == 1, far, NX - far), NX)

    def load(i):
        start = pl.multiple_of(slot_x(i) * COLS, COLS)
        return pltpu.make_async_copy(act.at[0, :, pl.ds(start, COLS)], act_v.at[i], load_sem.at[i])

    cot_load = pltpu.make_async_copy(cot.at[0], cot_v, small_sem.at[0])
    mom_load = pltpu.make_async_copy(mom.at[0], mom_v, small_sem.at[1])
    freq_load = pltpu.make_async_copy(freq, freq_v, small_sem.at[2])
    table_load = pltpu.make_async_copy(table, table_v, small_sem.at[3])
    cot_load.start()
    for i in range(NX):
        load(jnp.int32(i)).start()
    freq_load.start()
    table_load.start()
    mom_load.start()

    barrier = pltpu.get_barrier_semaphore()

    def hello(where):
        pl.semaphore_signal(barrier, inc=1, device_id=where, device_id_type=pl.DeviceIdType.MESH)

    def hello_group(j, carry):
        hello({"fsdp": me - core + 1, "dp": lax.rem(dp + j, NDP)})
        return carry

    def hello_ring(j, carry):
        hello({"fsdp": lax.rem(x + j, NX) * (2 * NY) + 2 * y})
        return carry

    lax.fori_loop(1, NX, hello_ring, 0)
    for rank in range(NY - 1):
        hello({"fsdp": 2 * (NY * x + ranked(rank))})

    @pl.when(core == 1)
    def _():
        hello({"fsdp": peer})

    lax.fori_loop(1, NDP, hello_group, 0)

    out_row = lax.broadcasted_iota(jnp.int32, (TOK, COLS), 0)
    in_col = lax.broadcasted_iota(jnp.int32, (TOK, COLS), 1)
    wanted = (out_row // BLOCK) * (2 * BLOCK) + out_row % BLOCK
    take_kept[...] = jnp.where(in_col == wanted + core * BLOCK, 1.0, 0.0).astype(BF16)
    take_sent[...] = jnp.where(in_col == wanted + (1 - core) * BLOCK, 1.0, 0.0).astype(BF16)

    def send(src, dst, send_sem, recv_sem, where):
        return pltpu.make_async_remote_copy(
            src_ref=src, dst_ref=dst, send_sem=send_sem, recv_sem=recv_sem,
            device_id=where, device_id_type=pl.DeviceIdType.MESH,
        )

    cot_copy = send(cot_send, cot_recv, cot_sem.at[0], cot_sem.at[1], {"fsdp": peer})

    def swap(i):
        return send(pick_send.at[i], pick_recv.at[i], core_send.at[i], core_recv.at[i], {"fsdp": peer})

    def pick(i):
        load(i).wait()
        pick_send[i] = dot(take_sent[...], act_v[i], 1, 1)

    def keep(i):
        kept[i] = dot(take_kept[...], act_v[i], 1, 1).astype(BF16)

    def first_half(way, rank):
        return (rank < 2) == (way == 0)

    def ax_copy(way, step, rank):
        raw = step == 1 or (step == 2 and not first_half(way, rank))
        return send(
            ga.at[slot_of(step, way), ranked(rank)] if raw else rax.at[way, step - 2, rank],
            rax.at[way, step - 1, rank],
            axs.at[way, step - 1, rank], axr.at[way, step - 1, rank], {"fsdp": around[way]},
        )

    def to_line(rank):
        return {"fsdp": me + 2 * (ranked(rank) - y)}

    def ay_copy(rank):
        return send(
            ga.at[NX - 1, ranked(rank)], ray.at[rank], ays.at[rank], ayr.at[rank], to_line(rank)
        )

    def by_copy(i, rank):
        return send(
            gb.at[i, ranked(rank)], rby.at[i, rank], bys.at[i, rank], byr.at[i, rank], to_line(rank)
        )

    def py_copy(i, rank):
        return send(
            pg.at[i, ranked(rank)], rpy.at[i, rank], pys.at[i, rank], pyr.at[i, rank], to_line(rank)
        )

    def px_copy(i):
        return send(
            psum.at[i], rpx.at[i], pxs.at[i], pxr.at[i],
            {"fsdp": slot_x(i) * (2 * NY) + base},
        )

    def dp_copy(to, slot):
        return send(pall.at[slot], pall.at[slot], dps.at[to], dpr.at[slot], {"dp": to})

    def bx_rows(way, step):
        if step > 1:
            return pl.ds(0, ROWS_B)
        return pl.ds(0, HALF_B) if way == 0 else pl.ds(HALF_B, ROWS_B - HALF_B)

    def bx_copy(way, step):
        rows = bx_rows(way, step)
        return send(
            rby.at[slot_of(step, way), 0, rows], rbx.at[way, step - 1, rows],
            bxs.at[way, step - 1], bxr.at[way, step - 1], {"fsdp": around[way]},
        )

    def product(i):
        total = dot(kept[i], cot_v[...])
        swap(i).wait_recv()
        total = total + dot(pick_recv[i].astype(BF16), cot_peer[...])
        blocks = total.reshape(NY, BLOCK, COLS)
        ga[i] = blocks[:, :ROWS_A]
        gb[i] = blocks[:, ROWS_A:]

    def by_start(i):
        for rank in range(NY - 1):
            by_copy(i, rank).start()

    cot_load.wait()
    cot_send[...] = cot_v[...].astype(F32)
    pick(jnp.int32(0))

    @pl.when(core == 0)
    def _():
        pl.semaphore_wait(barrier, 2 * (NX - 1) + 2 * (NY - 1) + 1)
        pl.semaphore_signal(
            gate.at[0], inc=1, device_id={"fsdp": peer}, device_id_type=pl.DeviceIdType.MESH
        )

    @pl.when(core == 1)
    def _():
        pl.semaphore_wait(gate.at[0], 1)

    cot_copy.start()
    swap(0).start()
    keep(0)
    for i in (1, 2):
        pick(jnp.int32(i))
        swap(i).start()
        keep(i)
    cot_copy.wait_recv()
    cot_peer[...] = cot_recv[...].astype(BF16)

    product(0)
    for rank in (0, 1):
        ax_copy(0, 1, rank).start()
        ax_copy(1, 1, rank + 2).start()
    by_start(0)
    product(1)
    for rank in (2, 3):
        ax_copy(0, 2, rank).start()
    product(2)
    for rank in (0, 1):
        ax_copy(1, 2, rank).start()
    by_start(1)
    by_start(2)

    def stage(i, carry):
        pick(i)
        swap(i).start()
        keep(i)
        return carry

    lax.fori_loop(3, NX, stage, 0)

    def finish(i, carry):
        product(i)
        return carry

    lax.fori_loop(3, NX, finish, 0)

    def choose():
        freq_load.wait()
        table_load.wait()
        wave = lax.broadcasted_iota(jnp.int32, (BLOCK, KEEP), 0)
        chosen = freq_v[...]
        hot_row = jnp.where(wave == chosen // BLOCK, 1.0, 0.0).astype(BF16)
        hot_col = jnp.where(wave == chosen % BLOCK, 1.0, 0.0).astype(BF16)
        rmix[...] = dot(hot_row, table_v[:, :256], 0, 0).astype(BF16)
        rinv[...] = dot(table_v[:, :128], hot_row, 0, 0).astype(BF16)
        pair = dot(hot_col, table_v[:, 256:], 0, 0)
        narrow = pair[:, :128] + pair[:, 128:]
        ltile[...] = jnp.concatenate([narrow] * 4, axis=1)

    def ax_part(way, step, rank):
        ax_copy(way, step - 1, rank).wait_recv()
        slot, sub = slot_of(step, way), ranked(rank)
        rax[way, step - 2, rank] = ga[slot, sub] + rax[way, step - 2, rank]
        ax_copy(way, step, rank).start()

    orders = {2: ((0, 1), (2, 3)), 3: ((2, 0, 3, 1), (0, 2, 1, 3)), 4: ((0, 2, 1, 3),) * 2, 5: ((0, 2, 1, 3),) * 2}

    def ax_round(step, place):
        if step <= 4:
            for way in (0, 1):
                ax_part(way, step, orders[step][way][place])
            return
        rank = orders[5][0][place]
        for way in (0, 1):
            ax_copy(way, 4, rank).wait_recv()
        sub = ranked(rank)
        ga[NX - 1, sub] = ga[NX - 1, sub] + (rax[0, 3, rank] + rax[1, 3, rank])
        if rank < 3:
            ay_copy(rank).start()

    def by_round(i):
        for rank in range(NY - 1):
            by_copy(i, rank).wait_recv()
        rby[i, 0] = gb[i, y] + rby[i, 0] + rby[i, 1] + rby[i, 2]

    def bx_round(i):
        if i == 0:
            bx_copy(0, 1).start()
            bx_copy(1, 1).start()
            return
        ways = (0, 1) if i == 7 else ((i + 1) % 2,)
        step = (i + 1) // 2 + 1
        for way in ways:
            bx_copy(way, step - 1).wait_recv()
            rows = bx_rows(way, step - 1)
            rby[i, 0, rows] = rby[i, 0, rows] + rbx[way, step - 2, rows]
            if step <= 4:
                bx_copy(way, step).start()

    block_row = lax.broadcasted_iota(jnp.int32, (8, COLS), 0)
    block_col = lax.broadcasted_iota(jnp.int32, (8, COLS), 1)
    ones = jnp.where(block_col // BLOCK == block_row, 1.0, 0.0).astype(BF16)

    def picks_of(rows):
        high, low = split(rows)
        spread = dot(rmix[...], jnp.concatenate([high, high, low, low], axis=0)) * ltile[...]
        high, low = split(spread)
        return dot(ones, high, 1, 1) + dot(ones, low, 1, 1)

    def back(values):
        high, low = split(values)
        wide = dot(jnp.concatenate([high, low], axis=0), jnp.concatenate([ones, ones], axis=0), 0, 0)
        high, low = split(wide * ltile[...])
        both = dot(rinv[...], high)
        return both[:BLOCK] + both[BLOCK:] + dot(rinv[:BLOCK, :], low)

    def partial(i, carry):
        for sub in range(NY):
            pg[i, sub] = picks_of(jnp.concatenate([ga[i, sub], gb[i, sub]], axis=0))
        for rank in range(NY - 1):
            py_copy(i, rank).start()
        return carry

    def partials(first):
        lax.fori_loop(first, first + 2, partial, 0)

    def line_sum(i, carry):
        for rank in range(NY - 1):
            py_copy(i, rank).wait_recv()
        psum[i] = pg[i, y] + rpy[i, 0] + rpy[i, 1] + rpy[i, 2]

        @pl.when(i < NX - 1)
        def _():
            px_copy(i).start()

        return carry

    def group_sum():
        total = psum[NX - 1] + picks_of(held[...])
        for i in range(NX - 1):
            px_copy(i).wait_recv()
            total = total + rpx[i]
        pall[dp] = total

        @pl.when(core == 1)
        def _():
            pl.semaphore_wait(barrier, 2 * (NDP - 1))
            pl.semaphore_signal(
                gate.at[1], inc=1, device_id={"fsdp": peer}, device_id_type=pl.DeviceIdType.MESH
            )

        @pl.when(core == 0)
        def _():
            pl.semaphore_wait(gate.at[1], 1)

        def share(j, carry):
            @pl.when(j != NDP // 2)
            def _():
                dp_copy(lax.rem(dp + NDP // 2 + j, NDP), dp).start()

            return carry

        lax.fori_loop(0, NDP, share, 0)
        held[...] = held[...] - back(total)

    choose()
    by_start(3)
    ax_round(2, 0)
    ax_round(2, 1)
    partials(0)
    by_start(4)
    ax_round(3, 0)
    partials(2)
    by_start(5)
    by_round(0)
    bx_round(0)
    ax_round(3, 1)
    ax_round(3, 2)
    ax_round(3, 3)
    partials(4)
    by_start(6)
    by_round(1)
    by_round(2)
    bx_round(1)
    bx_round(2)
    ax_round(4, 0)
    partials(6)
    by_start(7)
    mom_load.wait()
    held[...] = MOMENTUM_DECAY * mom_v[...]
    ax_round(4, 1)
    lax.fori_loop(0, NX, line_sum, 0)
    by_round(3)
    by_round(4)
    bx_round(3)
    bx_round(4)
    ax_round(4, 2)
    ax_round(4, 3)
    group_sum()
    by_round(5)
    by_round(6)
    bx_round(5)
    bx_round(6)
    by_round(7)
    for place in range(NY):
        ax_round(5, place)
    bx_round(7)
    for rank in (0, 2, 1):
        ay_copy(rank).wait_recv()
    gradient = jnp.concatenate([ga[NX - 1, y] + (ray[0] + ray[1] + ray[2]), rby[NX - 1, 0]], axis=0)
    newm[0] = held[...] + gradient

    def gather(j, carry):
        where = lax.rem(dp + j, NDP)
        dp_copy(where, where).wait_recv()
        return carry

    lax.fori_loop(1, NDP, gather, 0)
    upd[...] = back(jnp.sum(pall[...], axis=0) * (1.0 / NDP))

    cot_copy.wait_send()

    def done(i, carry):
        swap(i).wait_send()
        for rank in range(NY - 1):
            by_copy(i, rank).wait_send()
            py_copy(i, rank).wait_send()

        @pl.when(i < NX - 1)
        def _():
            px_copy(i).wait_send()

        return carry

    lax.fori_loop(0, NX, done, 0)
    for way in (0, 1):
        for step in range(1, 5):
            for rank in range(NY):
                if step > 1 or first_half(way, rank):
                    ax_copy(way, step, rank).wait_send()
            bx_copy(way, step).wait_send()
    for rank in range(NY - 1):
        ay_copy(rank).wait_send()

    def done_dp(j, carry):
        dp_copy(lax.rem(dp + j, NDP), dp).wait_send()
        return carry

    lax.fori_loop(1, NDP, done_dp, 0)


def shards(activations, cotangents, momentum, freq_index):
    vmem = pl.BlockSpec(memory_space=pltpu.VMEM)
    hbm = pl.BlockSpec(memory_space=pl.ANY)
    dma = pltpu.SemaphoreType.DMA
    return pl.pallas_call(
        kernel,
        out_shape=(
            jax.ShapeDtypeStruct((1, BLOCK, COLS), F32),
            jax.ShapeDtypeStruct((BLOCK, COLS), F32),
        ),
        in_specs=[hbm] * 5,
        out_specs=(vmem, vmem),
        scratch_shapes=[
            pltpu.VMEM((NX, TOK, COLS), BF16),
            pltpu.VMEM((TOK, COLS), BF16),
            pltpu.VMEM((BLOCK, COLS), F32),
            pltpu.VMEM((1, KEEP), jnp.int32),
            pltpu.VMEM((BLOCK, COLS), BF16),
            pltpu.VMEM((TOK, COLS), BF16),
            pltpu.VMEM((TOK, COLS), BF16),
            pltpu.VMEM((TOK, COLS), F32),
            pltpu.VMEM((TOK, COLS), F32),
            pltpu.VMEM((TOK, COLS), BF16),
            pltpu.VMEM((NX, NY * BLOCK, TOK), F32),
            pltpu.VMEM((NX, NY * BLOCK, TOK), F32),
            pltpu.VMEM((NX, NY * BLOCK, TOK), BF16),
            pltpu.VMEM((NX, NY, ROWS_A, COLS), F32),
            pltpu.VMEM((NX, NY, ROWS_B, COLS), F32),
            pltpu.VMEM((2, 4, NY, ROWS_A, COLS), F32),
            pltpu.VMEM((NY - 1, ROWS_A, COLS), F32),
            pltpu.VMEM((NX, NY - 1, ROWS_B, COLS), F32),
            pltpu.VMEM((2, 4, ROWS_B, COLS), F32),
            pltpu.VMEM((KEEP, 256), BF16),
            pltpu.VMEM((128, KEEP), BF16),
            pltpu.VMEM((KEEP, COLS), F32),
            pltpu.VMEM((BLOCK, COLS), F32),
            pltpu.VMEM((NX, NY, 8, KEEP), F32),
            pltpu.VMEM((NX, 8, KEEP), F32),
            pltpu.VMEM((NX, NY - 1, 8, KEEP), F32),
            pltpu.VMEM((NX - 1, 8, KEEP), F32),
            pltpu.VMEM((NDP, 8, KEEP), F32),
            pltpu.SemaphoreType.REGULAR((2,)),
            dma((NX,)), dma((4,)), dma((NX,)), dma((NX,)), dma((2,)),
            dma((2, 4, NY)), dma((2, 4, NY)),
            dma((NY - 1,)), dma((NY - 1,)),
            dma((NX, NY - 1)), dma((NX, NY - 1)),
            dma((2, 4)), dma((2, 4)),
            dma((NX, NY - 1)), dma((NX, NY - 1)), dma((NX - 1,)), dma((NX - 1,)),
            dma((NDP,)), dma((NDP,)),
        ],
        compiler_params=pltpu.CompilerParams(
            collective_id=0, has_side_effects=True, vmem_limit_bytes=62 * 1024 * 1024
        ),
    )(activations, cotangents, momentum, freq_index.reshape(1, KEEP), jnp.asarray(basis_tables()))


def solution(mesh):
    return jax.shard_map(
        shards,
        mesh=mesh,
        in_specs=(P("dp", "fsdp", None), P("dp", "fsdp", None), P("dp", "fsdp", None), P()),
        out_specs=(P("dp", "fsdp", None), P("fsdp", None)),
        check_vma=False,
    )
```

```python
import jax
import jax.numpy as jnp
import ml_dtypes
import numpy as np
from jax import lax
from jax.experimental import pallas as pl
from jax.experimental.pallas import tpu as pltpu
from jax.sharding import PartitionSpec as P

BLOCK = 64
KEEP = 256
NX = 8
NY = 4
NDP = 16
TOK = 256
COLS = 512
ROWS_A = 48
ROWS_B = BLOCK - ROWS_A
HALF_B = 8
MOMENTUM_DECAY = 0.999
BF16 = jnp.bfloat16
F32 = jnp.float32


def basis_tables():
    wave = np.arange(BLOCK)[:, None]
    sample = np.arange(BLOCK)[None, :]
    phase = ((2 * sample + 1) * wave) % (4 * BLOCK)
    scale = np.where(wave == 0, np.sqrt(1.0 / BLOCK), np.sqrt(2.0 / BLOCK))
    basis = scale * np.cos(np.pi * phase / (2.0 * BLOCK))
    high = basis.astype(ml_dtypes.bfloat16)
    low = (basis - high.astype(np.float64)).astype(ml_dtypes.bfloat16)
    return np.concatenate([high, low, high, low, high, high, low, low], axis=1)


def dot(lhs, rhs, left=1, right=0):
    return lax.dot_general(lhs, rhs, (((left,), (right,)), ((), ())), preferred_element_type=F32)


def split(values):
    high = values.astype(BF16)
    return high, (values - high.astype(F32)).astype(BF16)


def slot_of(step, way):
    if step == 1:
        return 0
    if step == 5:
        return 7
    return 2 * (step - 1) - 1 + way


def kernel(
    act, cot, mom, freq, table, newm, upd,
    act_v, cot_v, mom_v, freq_v, table_v, take_kept, take_sent, cot_send, cot_recv, cot_peer,
    pick_send, pick_recv, kept, ga, gb, rax, ray, rby, rbx,
    rmix, rinv, ltile, held, pg, psum, rpy, rpx, pall,
    gate, load_sem, small_sem, core_send, core_recv, cot_sem,
    axs, axr, ays, ayr, bys, byr, bxs, bxr, pys, pyr, pxs, pxr, dps, dpr,
):
    me = lax.axis_index("fsdp")
    dp = lax.axis_index("dp")
    x = me // (2 * NY)
    y = (me // 2) % NY
    core = me % 2
    base = me - 2 * NY * x
    peer = me + 1 - 2 * core
    around = (lax.rem(x + 1, NX) * (2 * NY) + base, lax.rem(x + NX - 1, NX) * (2 * NY) + base)

    def ranked(rank):
        return lax.rem(y + 1 + rank, NY)

    def slot_x(i):
        far = 4 - (i + 1) // 2
        return lax.rem(x + jnp.where(i % 2 == 1, far, NX - far), NX)

    def load(i):
        start = pl.multiple_of(slot_x(i) * COLS, COLS)
        return pltpu.make_async_copy(act.at[0, :, pl.ds(start, COLS)], act_v.at[i], load_sem.at[i])

    cot_load = pltpu.make_async_copy(cot.at[0], cot_v, small_sem.at[0])
    mom_load = pltpu.make_async_copy(mom.at[0], mom_v, small_sem.at[1])
    freq_load = pltpu.make_async_copy(freq, freq_v, small_sem.at[2])
    table_load = pltpu.make_async_copy(table, table_v, small_sem.at[3])
    cot_load.start()
    for i in range(NX):
        load(jnp.int32(i)).start()
    freq_load.start()
    table_load.start()
    mom_load.start()

    barrier = pltpu.get_barrier_semaphore()

    def hello(where):
        pl.semaphore_signal(barrier, inc=1, device_id=where, device_id_type=pl.DeviceIdType.MESH)

    def hello_group(j, carry):
        hello({"fsdp": me - core + 1, "dp": lax.rem(dp + j, NDP)})
        return carry

    def hello_ring(j, carry):
        hello({"fsdp": lax.rem(x + j, NX) * (2 * NY) + 2 * y})
        return carry

    lax.fori_loop(1, NX, hello_ring, 0)
    for rank in range(NY - 1):
        hello({"fsdp": 2 * (NY * x + ranked(rank))})

    @pl.when(core == 1)
    def _():
        hello({"fsdp": peer})

    lax.fori_loop(1, NDP, hello_group, 0)

    out_row = lax.broadcasted_iota(jnp.int32, (TOK, COLS), 0)
    in_col = lax.broadcasted_iota(jnp.int32, (TOK, COLS), 1)
    wanted = (out_row // BLOCK) * (2 * BLOCK) + out_row % BLOCK
    take_kept[...] = jnp.where(in_col == wanted + core * BLOCK, 1.0, 0.0).astype(BF16)
    take_sent[...] = jnp.where(in_col == wanted + (1 - core) * BLOCK, 1.0, 0.0).astype(BF16)

    def send(src, dst, send_sem, recv_sem, where):
        return pltpu.make_async_remote_copy(
            src_ref=src, dst_ref=dst, send_sem=send_sem, recv_sem=recv_sem,
            device_id=where, device_id_type=pl.DeviceIdType.MESH,
        )

    cot_copy = send(cot_send, cot_recv, cot_sem.at[0], cot_sem.at[1], {"fsdp": peer})

    def swap(i):
        return send(pick_send.at[i], pick_recv.at[i], core_send.at[i], core_recv.at[i], {"fsdp": peer})

    def pick(i):
        load(i).wait()
        pick_send[i] = dot(take_sent[...], act_v[i], 1, 1)

    def keep(i):
        kept[i] = dot(take_kept[...], act_v[i], 1, 1).astype(BF16)

    def first_half(way, rank):
        return (rank < 2) == (way == 0)

    def ax_copy(way, step, rank):
        raw = step == 1 or (step == 2 and not first_half(way, rank))
        return send(
            ga.at[slot_of(step, way), ranked(rank)] if raw else rax.at[way, step - 2, rank],
            rax.at[way, step - 1, rank],
            axs.at[way, step - 1, rank], axr.at[way, step - 1, rank], {"fsdp": around[way]},
        )

    def to_line(rank):
        return {"fsdp": me + 2 * (ranked(rank) - y)}

    def ay_copy(rank):
        return send(
            ga.at[NX - 1, ranked(rank)], ray.at[rank], ays.at[rank], ayr.at[rank], to_line(rank)
        )

    def by_copy(i, rank):
        return send(
            gb.at[i, ranked(rank)], rby.at[i, rank], bys.at[i, rank], byr.at[i, rank], to_line(rank)
        )

    def py_copy(i, rank):
        return send(
            pg.at[i, ranked(rank)], rpy.at[i, rank], pys.at[i, rank], pyr.at[i, rank], to_line(rank)
        )

    def px_copy(i):
        return send(
            psum.at[i], rpx.at[i], pxs.at[i], pxr.at[i],
            {"fsdp": slot_x(i) * (2 * NY) + base},
        )

    def dp_copy(to, slot):
        return send(pall.at[slot], pall.at[slot], dps.at[to], dpr.at[slot], {"dp": to})

    def bx_rows(way, step):
        if step > 1:
            return pl.ds(0, ROWS_B)
        return pl.ds(0, HALF_B) if way == 0 else pl.ds(HALF_B, ROWS_B - HALF_B)

    def bx_copy(way, step):
        rows = bx_rows(way, step)
        return send(
            rby.at[slot_of(step, way), 0, rows], rbx.at[way, step - 1, rows],
            bxs.at[way, step - 1], bxr.at[way, step - 1], {"fsdp": around[way]},
        )

    def product(i):
        total = dot(kept[i], cot_v[...])
        swap(i).wait_recv()
        total = total + dot(pick_recv[i].astype(BF16), cot_peer[...])
        blocks = total.reshape(NY, BLOCK, COLS)
        ga[i] = blocks[:, :ROWS_A]
        gb[i] = blocks[:, ROWS_A:]

    def by_start(i):
        for rank in range(NY - 1):
            by_copy(i, rank).start()

    cot_load.wait()
    cot_send[...] = cot_v[...].astype(F32)
    pick(jnp.int32(0))

    @pl.when(core == 0)
    def _():
        pl.semaphore_wait(barrier, 2 * (NX - 1) + 2 * (NY - 1) + 1)
        pl.semaphore_signal(
            gate.at[0], inc=1, device_id={"fsdp": peer}, device_id_type=pl.DeviceIdType.MESH
        )

    @pl.when(core == 1)
    def _():
        pl.semaphore_wait(gate.at[0], 1)

    cot_copy.start()
    swap(0).start()
    keep(0)
    for i in (1, 2):
        pick(jnp.int32(i))
        swap(i).start()
        keep(i)
    cot_copy.wait_recv()
    cot_peer[...] = cot_recv[...].astype(BF16)

    product(0)
    for rank in (0, 1):
        ax_copy(0, 1, rank).start()
        ax_copy(1, 1, rank + 2).start()
    by_start(0)
    product(1)
    for rank in (2, 3):
        ax_copy(0, 2, rank).start()
    product(2)
    for rank in (0, 1):
        ax_copy(1, 2, rank).start()
    by_start(1)
    by_start(2)

    def stage(i, carry):
        pick(i)
        swap(i).start()
        keep(i)
        return carry

    lax.fori_loop(3, NX, stage, 0)

    def finish(i, carry):
        product(i)
        return carry

    lax.fori_loop(3, NX, finish, 0)

    def choose():
        freq_load.wait()
        table_load.wait()
        wave = lax.broadcasted_iota(jnp.int32, (BLOCK, KEEP), 0)
        chosen = freq_v[...]
        hot_row = jnp.where(wave == chosen // BLOCK, 1.0, 0.0).astype(BF16)
        hot_col = jnp.where(wave == chosen % BLOCK, 1.0, 0.0).astype(BF16)
        rmix[...] = dot(hot_row, table_v[:, :256], 0, 0).astype(BF16)
        rinv[...] = dot(table_v[:, :128], hot_row, 0, 0).astype(BF16)
        pair = dot(hot_col, table_v[:, 256:], 0, 0)
        narrow = pair[:, :128] + pair[:, 128:]
        ltile[...] = jnp.concatenate([narrow] * 4, axis=1)

    def ax_part(way, step, rank):
        ax_copy(way, step - 1, rank).wait_recv()
        slot, sub = slot_of(step, way), ranked(rank)
        rax[way, step - 2, rank] = ga[slot, sub] + rax[way, step - 2, rank]
        ax_copy(way, step, rank).start()

    orders = {2: ((0, 1), (2, 3)), 3: ((2, 0, 3, 1), (0, 2, 1, 3)), 4: ((0, 2, 1, 3),) * 2, 5: ((0, 2, 1, 3),) * 2}

    def ax_round(step, place):
        if step <= 4:
            for way in (0, 1):
                ax_part(way, step, orders[step][way][place])
            return
        rank = orders[5][0][place]
        for way in (0, 1):
            ax_copy(way, 4, rank).wait_recv()
        sub = ranked(rank)
        ga[NX - 1, sub] = ga[NX - 1, sub] + (rax[0, 3, rank] + rax[1, 3, rank])
        if rank < 3:
            ay_copy(rank).start()

    def by_round(i):
        for rank in range(NY - 1):
            by_copy(i, rank).wait_recv()
        rby[i, 0] = gb[i, y] + rby[i, 0] + rby[i, 1] + rby[i, 2]

    def bx_round(i):
        if i == 0:
            bx_copy(0, 1).start()
            bx_copy(1, 1).start()
            return
        ways = (0, 1) if i == 7 else ((i + 1) % 2,)
        step = (i + 1) // 2 + 1
        for way in ways:
            bx_copy(way, step - 1).wait_recv()
            rows = bx_rows(way, step - 1)
            rby[i, 0, rows] = rby[i, 0, rows] + rbx[way, step - 2, rows]
            if step <= 4:
                bx_copy(way, step).start()

    block_row = lax.broadcasted_iota(jnp.int32, (8, COLS), 0)
    block_col = lax.broadcasted_iota(jnp.int32, (8, COLS), 1)
    ones = jnp.where(block_col // BLOCK == block_row, 1.0, 0.0).astype(BF16)

    def picks_of(rows):
        high, low = split(rows)
        spread = dot(rmix[...], jnp.concatenate([high, high, low, low], axis=0)) * ltile[...]
        high, low = split(spread)
        return dot(ones, high, 1, 1) + dot(ones, low, 1, 1)

    def back(values):
        high, low = split(values)
        wide = dot(jnp.concatenate([high, low], axis=0), jnp.concatenate([ones, ones], axis=0), 0, 0)
        high, low = split(wide * ltile[...])
        both = dot(rinv[...], high)
        return both[:BLOCK] + both[BLOCK:] + dot(rinv[:BLOCK, :], low)

    def partial(i, carry):
        for sub in range(NY):
            pg[i, sub] = picks_of(jnp.concatenate([ga[i, sub], gb[i, sub]], axis=0))
        for rank in range(NY - 1):
            py_copy(i, rank).start()
        return carry

    def partials(first):
        lax.fori_loop(first, first + 2, partial, 0)

    def line_sum(i, carry):
        for rank in range(NY - 1):
            py_copy(i, rank).wait_recv()
        psum[i] = pg[i, y] + rpy[i, 0] + rpy[i, 1] + rpy[i, 2]

        @pl.when(i < NX - 1)
        def _():
            px_copy(i).start()

        return carry

    def group_sum():
        total = psum[NX - 1] + picks_of(held[...])
        for i in range(NX - 1):
            px_copy(i).wait_recv()
            total = total + rpx[i]
        pall[dp] = total

        @pl.when(core == 1)
        def _():
            pl.semaphore_wait(barrier, 2 * (NDP - 1))
            pl.semaphore_signal(
                gate.at[1], inc=1, device_id={"fsdp": peer}, device_id_type=pl.DeviceIdType.MESH
            )

        @pl.when(core == 0)
        def _():
            pl.semaphore_wait(gate.at[1], 1)

        def share(j, carry):
            @pl.when(j != NDP // 2)
            def _():
                dp_copy(lax.rem(dp + NDP // 2 + j, NDP), dp).start()

            return carry

        lax.fori_loop(0, NDP, share, 0)
        held[...] = held[...] - back(total)

    choose()
    ax_round(2, 0)
    ax_round(2, 1)
    partials(0)
    ax_round(3, 0)
    partials(2)
    by_start(3)
    ax_round(3, 1)
    partials(4)
    by_start(4)
    ax_round(3, 2)
    ax_round(3, 3)
    by_round(0)
    bx_round(0)
    partials(6)
    by_start(5)
    mom_load.wait()
    held[...] = MOMENTUM_DECAY * mom_v[...]
    lax.fori_loop(0, NX, line_sum, 0)
    by_start(6)
    by_round(1)
    bx_round(1)
    by_round(2)
    bx_round(2)
    ax_round(4, 0)
    ax_round(4, 1)
    by_start(7)
    group_sum()
    by_round(3)
    by_round(4)
    bx_round(3)
    bx_round(4)
    ax_round(4, 2)
    ax_round(4, 3)
    by_round(5)
    by_round(6)
    bx_round(5)
    bx_round(6)
    by_round(7)
    for place in range(NY):
        ax_round(5, place)
    bx_round(7)
    for rank in (0, 2, 1):
        ay_copy(rank).wait_recv()
    gradient = jnp.concatenate([ga[NX - 1, y] + (ray[0] + ray[1] + ray[2]), rby[NX - 1, 0]], axis=0)
    newm[0] = held[...] + gradient

    def gather(j, carry):
        where = lax.rem(dp + j, NDP)
        dp_copy(where, where).wait_recv()
        return carry

    lax.fori_loop(1, NDP, gather, 0)
    upd[...] = back(jnp.sum(pall[...], axis=0) * (1.0 / NDP))

    cot_copy.wait_send()

    def done(i, carry):
        swap(i).wait_send()
        for rank in range(NY - 1):
            by_copy(i, rank).wait_send()
            py_copy(i, rank).wait_send()

        @pl.when(i < NX - 1)
        def _():
            px_copy(i).wait_send()

        return carry

    lax.fori_loop(0, NX, done, 0)
    for way in (0, 1):
        for step in range(1, 5):
            for rank in range(NY):
                if step > 1 or first_half(way, rank):
                    ax_copy(way, step, rank).wait_send()
            bx_copy(way, step).wait_send()
    for rank in range(NY - 1):
        ay_copy(rank).wait_send()

    def done_dp(j, carry):
        dp_copy(lax.rem(dp + j, NDP), dp).wait_send()
        return carry

    lax.fori_loop(1, NDP, done_dp, 0)


def shards(activations, cotangents, momentum, freq_index):
    vmem = pl.BlockSpec(memory_space=pltpu.VMEM)
    hbm = pl.BlockSpec(memory_space=pl.ANY)
    dma = pltpu.SemaphoreType.DMA
    return pl.pallas_call(
        kernel,
        out_shape=(
            jax.ShapeDtypeStruct((1, BLOCK, COLS), F32),
            jax.ShapeDtypeStruct((BLOCK, COLS), F32),
        ),
        in_specs=[hbm] * 5,
        out_specs=(vmem, vmem),
        scratch_shapes=[
            pltpu.VMEM((NX, TOK, COLS), BF16),
            pltpu.VMEM((TOK, COLS), BF16),
            pltpu.VMEM((BLOCK, COLS), F32),
            pltpu.VMEM((1, KEEP), jnp.int32),
            pltpu.VMEM((BLOCK, COLS), BF16),
            pltpu.VMEM((TOK, COLS), BF16),
            pltpu.VMEM((TOK, COLS), BF16),
            pltpu.VMEM((TOK, COLS), F32),
            pltpu.VMEM((TOK, COLS), F32),
            pltpu.VMEM((TOK, COLS), BF16),
            pltpu.VMEM((NX, NY * BLOCK, TOK), F32),
            pltpu.VMEM((NX, NY * BLOCK, TOK), F32),
            pltpu.VMEM((NX, NY * BLOCK, TOK), BF16),
            pltpu.VMEM((NX, NY, ROWS_A, COLS), F32),
            pltpu.VMEM((NX, NY, ROWS_B, COLS), F32),
            pltpu.VMEM((2, 4, NY, ROWS_A, COLS), F32),
            pltpu.VMEM((NY - 1, ROWS_A, COLS), F32),
            pltpu.VMEM((NX, NY - 1, ROWS_B, COLS), F32),
            pltpu.VMEM((2, 4, ROWS_B, COLS), F32),
            pltpu.VMEM((KEEP, 256), BF16),
            pltpu.VMEM((128, KEEP), BF16),
            pltpu.VMEM((KEEP, COLS), F32),
            pltpu.VMEM((BLOCK, COLS), F32),
            pltpu.VMEM((NX, NY, 8, KEEP), F32),
            pltpu.VMEM((NX, 8, KEEP), F32),
            pltpu.VMEM((NX, NY - 1, 8, KEEP), F32),
            pltpu.VMEM((NX - 1, 8, KEEP), F32),
            pltpu.VMEM((NDP, 8, KEEP), F32),
            pltpu.SemaphoreType.REGULAR((2,)),
            dma((NX,)), dma((4,)), dma((NX,)), dma((NX,)), dma((2,)),
            dma((2, 4, NY)), dma((2, 4, NY)),
            dma((NY - 1,)), dma((NY - 1,)),
            dma((NX, NY - 1)), dma((NX, NY - 1)),
            dma((2, 4)), dma((2, 4)),
            dma((NX, NY - 1)), dma((NX, NY - 1)), dma((NX - 1,)), dma((NX - 1,)),
            dma((NDP,)), dma((NDP,)),
        ],
        compiler_params=pltpu.CompilerParams(
            collective_id=0, has_side_effects=True, vmem_limit_bytes=62 * 1024 * 1024
        ),
    )(activations, cotangents, momentum, freq_index.reshape(1, KEEP), jnp.asarray(basis_tables()))


def solution(mesh):
    return jax.shard_map(
        shards,
        mesh=mesh,
        in_specs=(P("dp", "fsdp", None), P("dp", "fsdp", None), P("dp", "fsdp", None), P()),
        out_specs=(P("dp", "fsdp", None), P("fsdp", None)),
        check_vma=False,
    )
```

```python
import jax
import jax.numpy as jnp
import ml_dtypes
import numpy as np
from jax import lax
from jax.experimental import pallas as pl
from jax.experimental.pallas import tpu as pltpu
from jax.sharding import PartitionSpec as P

BLOCK = 64
KEEP = 256
NX = 8
NY = 4
NDP = 16
TOK = 256
COLS = 512
ROWS_A = 48
ROWS_B = BLOCK - ROWS_A
HALF_B = 8
MOMENTUM_DECAY = 0.999
BF16 = jnp.bfloat16
F32 = jnp.float32


def basis_tables():
    wave = np.arange(BLOCK)[:, None]
    sample = np.arange(BLOCK)[None, :]
    phase = ((2 * sample + 1) * wave) % (4 * BLOCK)
    scale = np.where(wave == 0, np.sqrt(1.0 / BLOCK), np.sqrt(2.0 / BLOCK))
    basis = scale * np.cos(np.pi * phase / (2.0 * BLOCK))
    high = basis.astype(ml_dtypes.bfloat16)
    low = (basis - high.astype(np.float64)).astype(ml_dtypes.bfloat16)
    return np.concatenate([high, low, high, low, high, high, low, low], axis=1)


def dot(lhs, rhs, left=1, right=0):
    return lax.dot_general(lhs, rhs, (((left,), (right,)), ((), ())), preferred_element_type=F32)


def split(values):
    high = values.astype(BF16)
    return high, (values - high.astype(F32)).astype(BF16)


def slot_of(step, way):
    if step == 1:
        return 0
    if step == 5:
        return 7
    return 2 * (step - 1) - 1 + way


def kernel(
    act, cot, mom, freq, table, both_out,
    act_v, cot_v, mom_v, freq_v, table_v, take_kept, take_sent, cot_send, cot_recv, cot_peer,
    pick_send, pick_recv, kept, ga, gb, rax, ray, rby, rbx,
    rmix, rinv, ltile, held, pg, psum, rpy, rpx, pall,
    gate, load_sem, small_sem, core_send, core_recv, cot_sem,
    axs, axr, ays, ayr, bys, byr, bxs, bxr, pys, pyr, pxs, pxr, dps, dpr,
):
    me = lax.axis_index("fsdp")
    dp = lax.axis_index("dp")
    x = me // (2 * NY)
    y = (me // 2) % NY
    core = me % 2
    base = me - 2 * NY * x
    peer = me + 1 - 2 * core
    around = (lax.rem(x + 1, NX) * (2 * NY) + base, lax.rem(x + NX - 1, NX) * (2 * NY) + base)

    def ranked(rank):
        return lax.rem(y + 1 + rank, NY)

    def slot_x(i):
        far = 4 - (i + 1) // 2
        return lax.rem(x + jnp.where(i % 2 == 1, far, NX - far), NX)

    def load(i):
        start = pl.multiple_of(slot_x(i) * COLS, COLS)
        return pltpu.make_async_copy(act.at[0, :, pl.ds(start, COLS)], act_v.at[i], load_sem.at[i])

    cot_load = pltpu.make_async_copy(cot.at[0], cot_v, small_sem.at[0])
    mom_load = pltpu.make_async_copy(mom.at[0], mom_v, small_sem.at[1])
    freq_load = pltpu.make_async_copy(freq, freq_v, small_sem.at[2])
    table_load = pltpu.make_async_copy(table, table_v, small_sem.at[3])
    cot_load.start()
    for i in range(NX):
        load(jnp.int32(i)).start()
    freq_load.start()
    table_load.start()
    mom_load.start()

    barrier = pltpu.get_barrier_semaphore()

    def hello(where):
        pl.semaphore_signal(barrier, inc=1, device_id=where, device_id_type=pl.DeviceIdType.MESH)

    def hello_group(j, carry):
        hello({"fsdp": me - core + 1, "dp": lax.rem(dp + j, NDP)})
        return carry

    def hello_ring(j, carry):
        hello({"fsdp": lax.rem(x + j, NX) * (2 * NY) + 2 * y})
        return carry

    lax.fori_loop(1, NX, hello_ring, 0)
    for rank in range(NY - 1):
        hello({"fsdp": 2 * (NY * x + ranked(rank))})

    @pl.when(core == 1)
    def _():
        hello({"fsdp": peer})

    lax.fori_loop(1, NDP, hello_group, 0)

    out_row = lax.broadcasted_iota(jnp.int32, (TOK, COLS), 0)
    in_col = lax.broadcasted_iota(jnp.int32, (TOK, COLS), 1)
    wanted = (out_row // BLOCK) * (2 * BLOCK) + out_row % BLOCK
    take_kept[...] = jnp.where(in_col == wanted + core * BLOCK, 1.0, 0.0).astype(BF16)
    take_sent[...] = jnp.where(in_col == wanted + (1 - core) * BLOCK, 1.0, 0.0).astype(BF16)

    def send(src, dst, send_sem, recv_sem, where):
        return pltpu.make_async_remote_copy(
            src_ref=src, dst_ref=dst, send_sem=send_sem, recv_sem=recv_sem,
            device_id=where, device_id_type=pl.DeviceIdType.MESH,
        )

    cot_copy = send(cot_send, cot_recv, cot_sem.at[0], cot_sem.at[1], {"fsdp": peer})

    def swap(i):
        return send(pick_send.at[i], pick_recv.at[i], core_send.at[i], core_recv.at[i], {"fsdp": peer})

    def pick(i):
        load(i).wait()
        pick_send[i] = dot(take_sent[...], act_v[i], 1, 1)

    def keep(i):
        kept[i] = dot(take_kept[...], act_v[i], 1, 1).astype(BF16)

    def first_half(way, rank):
        return (rank < 2) == (way == 0)

    def ax_copy(way, step, rank):
        raw = step == 1 or (step == 2 and not first_half(way, rank))
        return send(
            ga.at[slot_of(step, way), ranked(rank)] if raw else rax.at[way, step - 2, rank],
            rax.at[way, step - 1, rank],
            axs.at[way, step - 1, rank], axr.at[way, step - 1, rank], {"fsdp": around[way]},
        )

    def to_line(rank):
        return {"fsdp": me + 2 * (ranked(rank) - y)}

    def ay_copy(rank):
        return send(
            ga.at[NX - 1, ranked(rank)], ray.at[rank], ays.at[rank], ayr.at[rank], to_line(rank)
        )

    def by_copy(i, rank):
        return send(
            gb.at[i, ranked(rank)], rby.at[i, rank], bys.at[i, rank], byr.at[i, rank], to_line(rank)
        )

    def py_copy(i, rank):
        return send(
            pg.at[i, ranked(rank)], rpy.at[i, rank], pys.at[i, rank], pyr.at[i, rank], to_line(rank)
        )

    def px_copy(i):
        return send(
            psum.at[i], rpx.at[i], pxs.at[i], pxr.at[i],
            {"fsdp": slot_x(i) * (2 * NY) + base},
        )

    def dp_copy(to, slot):
        return send(pall.at[slot], pall.at[slot], dps.at[to], dpr.at[slot], {"dp": to})

    def bx_rows(way, step):
        if step > 1:
            return pl.ds(0, ROWS_B)
        return pl.ds(0, HALF_B) if way == 0 else pl.ds(HALF_B, ROWS_B - HALF_B)

    def bx_copy(way, step):
        rows = bx_rows(way, step)
        return send(
            rby.at[slot_of(step, way), 0, rows], rbx.at[way, step - 1, rows],
            bxs.at[way, step - 1], bxr.at[way, step - 1], {"fsdp": around[way]},
        )

    def product(i):
        total = dot(kept[i], cot_v[...])
        swap(i).wait_recv()
        total = total + dot(pick_recv[i].astype(BF16), cot_peer[...])
        blocks = total.reshape(NY, BLOCK, COLS)
        ga[i] = blocks[:, :ROWS_A]
        gb[i] = blocks[:, ROWS_A:]

    def by_start(i):
        for rank in range(NY - 1):
            by_copy(i, rank).start()

    cot_load.wait()
    cot_send[...] = cot_v[...].astype(F32)
    pick(jnp.int32(0))

    @pl.when(core == 0)
    def _():
        pl.semaphore_wait(barrier, 2 * (NX - 1) + 2 * (NY - 1) + 1)
        pl.semaphore_signal(
            gate.at[0], inc=1, device_id={"fsdp": peer}, device_id_type=pl.DeviceIdType.MESH
        )

    @pl.when(core == 1)
    def _():
        pl.semaphore_wait(gate.at[0], 1)

    cot_copy.start()
    swap(0).start()
    keep(0)
    for i in (1, 2):
        pick(jnp.int32(i))
        swap(i).start()
        keep(i)
    cot_copy.wait_recv()
    cot_peer[...] = cot_recv[...].astype(BF16)

    product(0)
    for rank in (0, 1):
        ax_copy(0, 1, rank).start()
        ax_copy(1, 1, rank + 2).start()
    by_start(0)
    product(1)
    for rank in (2, 3):
        ax_copy(0, 2, rank).start()
    product(2)
    for rank in (0, 1):
        ax_copy(1, 2, rank).start()
    by_start(1)
    by_start(2)

    def stage(i, carry):
        pick(i)
        swap(i).start()
        keep(i)
        return carry

    lax.fori_loop(3, NX, stage, 0)

    def finish(i, carry):
        product(i)
        return carry

    lax.fori_loop(3, NX, finish, 0)

    def choose():
        freq_load.wait()
        table_load.wait()
        wave = lax.broadcasted_iota(jnp.int32, (BLOCK, KEEP), 0)
        chosen = freq_v[...]
        hot_row = jnp.where(wave == chosen // BLOCK, 1.0, 0.0).astype(BF16)
        hot_col = jnp.where(wave == chosen % BLOCK, 1.0, 0.0).astype(BF16)
        rmix[...] = dot(hot_row, table_v[:, :256], 0, 0).astype(BF16)
        rinv[...] = dot(table_v[:, :128], hot_row, 0, 0).astype(BF16)
        pair = dot(hot_col, table_v[:, 256:], 0, 0)
        narrow = pair[:, :128] + pair[:, 128:]
        ltile[...] = jnp.concatenate([narrow] * 4, axis=1)

    def ax_part(way, step, rank):
        ax_copy(way, step - 1, rank).wait_recv()
        slot, sub = slot_of(step, way), ranked(rank)
        rax[way, step - 2, rank] = ga[slot, sub] + rax[way, step - 2, rank]
        ax_copy(way, step, rank).start()

    orders = {2: ((0, 1), (2, 3)), 3: ((2, 0, 3, 1), (0, 2, 1, 3)), 4: ((0, 2, 1, 3),) * 2, 5: ((0, 2, 1, 3),) * 2}

    def ax_round(step, place):
        if step <= 4:
            for way in (0, 1):
                ax_part(way, step, orders[step][way][place])
            return
        rank = orders[5][0][place]
        for way in (0, 1):
            ax_copy(way, 4, rank).wait_recv()
        sub = ranked(rank)
        ga[NX - 1, sub] = ga[NX - 1, sub] + (rax[0, 3, rank] + rax[1, 3, rank])
        if rank < 3:
            ay_copy(rank).start()

    def by_round(i):
        for rank in range(NY - 1):
            by_copy(i, rank).wait_recv()
        rby[i, 0] = gb[i, y] + rby[i, 0] + rby[i, 1] + rby[i, 2]

    def bx_round(i):
        if i == 0:
            bx_copy(0, 1).start()
            bx_copy(1, 1).start()
            return
        ways = (0, 1) if i == 7 else ((i + 1) % 2,)
        step = (i + 1) // 2 + 1
        for way in ways:
            bx_copy(way, step - 1).wait_recv()
            rows = bx_rows(way, step - 1)
            rby[i, 0, rows] = rby[i, 0, rows] + rbx[way, step - 2, rows]
            if step <= 4:
                bx_copy(way, step).start()

    block_row = lax.broadcasted_iota(jnp.int32, (8, COLS), 0)
    block_col = lax.broadcasted_iota(jnp.int32, (8, COLS), 1)
    ones = jnp.where(block_col // BLOCK == block_row, 1.0, 0.0).astype(BF16)

    def picks_of(rows):
        high, low = split(rows)
        spread = dot(rmix[...], jnp.concatenate([high, high, low, low], axis=0)) * ltile[...]
        high, low = split(spread)
        return dot(ones, high, 1, 1) + dot(ones, low, 1, 1)

    def back(values):
        high, low = split(values)
        wide = dot(jnp.concatenate([high, low], axis=0), jnp.concatenate([ones, ones], axis=0), 0, 0)
        high, low = split(wide * ltile[...])
        both = dot(rinv[...], high)
        return both[:BLOCK] + both[BLOCK:] + dot(rinv[:BLOCK, :], low)

    def partial(i, carry):
        for sub in range(NY):
            pg[i, sub] = picks_of(jnp.concatenate([ga[i, sub], gb[i, sub]], axis=0))
        for rank in range(NY - 1):
            py_copy(i, rank).start()
        return carry

    def partials(first):
        lax.fori_loop(first, first + 2, partial, 0)

    def line_sum(i, carry):
        for rank in range(NY - 1):
            py_copy(i, rank).wait_recv()
        psum[i] = pg[i, y] + rpy[i, 0] + rpy[i, 1] + rpy[i, 2]

        @pl.when(i < NX - 1)
        def _():
            px_copy(i).start()

        return carry

    def group_sum():
        total = psum[NX - 1] + picks_of(held[...])
        for i in range(NX - 1):
            px_copy(i).wait_recv()
            total = total + rpx[i]
        pall[dp] = total

        @pl.when(core == 1)
        def _():
            pl.semaphore_wait(barrier, 2 * (NDP - 1))
            pl.semaphore_signal(
                gate.at[1], inc=1, device_id={"fsdp": peer}, device_id_type=pl.DeviceIdType.MESH
            )

        @pl.when(core == 0)
        def _():
            pl.semaphore_wait(gate.at[1], 1)

        def share(j, carry):
            @pl.when(j != NDP // 2)
            def _():
                dp_copy(lax.rem(dp + NDP // 2 + j, NDP), dp).start()

            return carry

        lax.fori_loop(0, NDP, share, 0)
        held[...] = held[...] - back(total)

    choose()
    ax_round(2, 0)
    ax_round(2, 1)
    partials(0)
    ax_round(3, 0)
    partials(2)
    by_start(3)
    ax_round(3, 1)
    partials(4)
    by_start(4)
    ax_round(3, 2)
    ax_round(3, 3)
    by_round(0)
    bx_round(0)
    lax.fori_loop(0, 4, line_sum, 0)
    partials(6)
    by_start(5)
    mom_load.wait()
    held[...] = MOMENTUM_DECAY * mom_v[...]
    lax.fori_loop(4, NX, line_sum, 0)
    by_start(6)
    by_round(1)
    bx_round(1)
    by_round(2)
    bx_round(2)
    ax_round(4, 0)
    ax_round(4, 1)
    by_start(7)
    group_sum()
    by_round(3)
    by_round(4)
    bx_round(3)
    bx_round(4)
    ax_round(4, 2)
    ax_round(4, 3)
    by_round(5)
    by_round(6)
    bx_round(5)
    bx_round(6)
    by_round(7)
    cot_copy.wait_send()

    def done(i, carry):
        swap(i).wait_send()
        for rank in range(NY - 1):
            by_copy(i, rank).wait_send()
            py_copy(i, rank).wait_send()

        @pl.when(i < NX - 1)
        def _():
            px_copy(i).wait_send()

        return carry

    def done_ring(first, last):
        for way in (0, 1):
            for step in range(first, last + 1):
                for rank in range(NY):
                    if step > 1 or first_half(way, rank):
                        ax_copy(way, step, rank).wait_send()
                bx_copy(way, step).wait_send()

    def done_dp(j, carry):
        dp_copy(lax.rem(dp + j, NDP), dp).wait_send()
        return carry

    lax.fori_loop(0, NX, done, 0)
    lax.fori_loop(1, NDP, done_dp, 0)
    done_ring(1, 2)
    for place in range(NY):
        ax_round(5, place)
    bx_round(7)
    for rank in (0, 2, 1):
        ay_copy(rank).wait_recv()
    gradient = jnp.concatenate([ga[NX - 1, y] + (ray[0] + ray[1] + ray[2]), rby[NX - 1, 0]], axis=0)
    both_out[0] = held[...] + gradient
    done_ring(3, 4)
    for rank in range(NY - 1):
        ay_copy(rank).wait_send()

    def gather(j, carry):
        where = lax.rem(dp + j, NDP)
        dp_copy(where, where).wait_recv()
        return carry

    lax.fori_loop(1, NDP, gather, 0)
    both_out[1] = back(jnp.sum(pall[...], axis=0) * (1.0 / NDP))


def shards(activations, cotangents, momentum, freq_index):
    vmem = pl.BlockSpec(memory_space=pltpu.VMEM)
    hbm = pl.BlockSpec(memory_space=pl.ANY)
    dma = pltpu.SemaphoreType.DMA
    result = pl.pallas_call(
        kernel,
        out_shape=jax.ShapeDtypeStruct((2, BLOCK, COLS), F32),
        in_specs=[hbm] * 5,
        out_specs=vmem,
        scratch_shapes=[
            pltpu.VMEM((NX, TOK, COLS), BF16),
            pltpu.VMEM((TOK, COLS), BF16),
            pltpu.VMEM((BLOCK, COLS), F32),
            pltpu.VMEM((1, KEEP), jnp.int32),
            pltpu.VMEM((BLOCK, COLS), BF16),
            pltpu.VMEM((TOK, COLS), BF16),
            pltpu.VMEM((TOK, COLS), BF16),
            pltpu.VMEM((TOK, COLS), F32),
            pltpu.VMEM((TOK, COLS), F32),
            pltpu.VMEM((TOK, COLS), BF16),
            pltpu.VMEM((NX, NY * BLOCK, TOK), F32),
            pltpu.VMEM((NX, NY * BLOCK, TOK), F32),
            pltpu.VMEM((NX, NY * BLOCK, TOK), BF16),
            pltpu.VMEM((NX, NY, ROWS_A, COLS), F32),
            pltpu.VMEM((NX, NY, ROWS_B, COLS), F32),
            pltpu.VMEM((2, 4, NY, ROWS_A, COLS), F32),
            pltpu.VMEM((NY - 1, ROWS_A, COLS), F32),
            pltpu.VMEM((NX, NY - 1, ROWS_B, COLS), F32),
            pltpu.VMEM((2, 4, ROWS_B, COLS), F32),
            pltpu.VMEM((KEEP, 256), BF16),
            pltpu.VMEM((128, KEEP), BF16),
            pltpu.VMEM((KEEP, COLS), F32),
            pltpu.VMEM((BLOCK, COLS), F32),
            pltpu.VMEM((NX, NY, 8, KEEP), F32),
            pltpu.VMEM((NX, 8, KEEP), F32),
            pltpu.VMEM((NX, NY - 1, 8, KEEP), F32),
            pltpu.VMEM((NX - 1, 8, KEEP), F32),
            pltpu.VMEM((NDP, 8, KEEP), F32),
            pltpu.SemaphoreType.REGULAR((2,)),
            dma((NX,)), dma((4,)), dma((NX,)), dma((NX,)), dma((2,)),
            dma((2, 4, NY)), dma((2, 4, NY)),
            dma((NY - 1,)), dma((NY - 1,)),
            dma((NX, NY - 1)), dma((NX, NY - 1)),
            dma((2, 4)), dma((2, 4)),
            dma((NX, NY - 1)), dma((NX, NY - 1)), dma((NX - 1,)), dma((NX - 1,)),
            dma((NDP,)), dma((NDP,)),
        ],
        compiler_params=pltpu.CompilerParams(
            collective_id=0, has_side_effects=True, vmem_limit_bytes=62 * 1024 * 1024
        ),
    )(activations, cotangents, momentum, freq_index.reshape(1, KEEP), jnp.asarray(basis_tables()))
    return result[:1], result[1]


def solution(mesh):
    return jax.shard_map(
        shards,
        mesh=mesh,
        in_specs=(P("dp", "fsdp", None), P("dp", "fsdp", None), P("dp", "fsdp", None), P()),
        out_specs=(P("dp", "fsdp", None), P("fsdp", None)),
        check_vma=False,
    )
```
